256 devices in a mesh: mp: 16 (over z, core), hidden: 16 (over y, x).
Axes of the slice: x: 4, y: 4, z: 8, core: 2. Of those that a mesh axis runs over, the one named last changes fastest.
Arguments:
- tokens: bfloat16 [512, 8192], P('hidden', 'mp'), may hold values from -6 to 6
- grad_output: bfloat16 [512, 8192], P('hidden', 'mp'), may hold values from -6 to 6
- gate_weight: bfloat16 [8192, 28672], P('mp', 'hidden'), may hold values from -0.0625 to 0.0625
- up_weight: bfloat16 [8192, 28672], P('mp', 'hidden'), may hold values from -0.0625 to 0.0625
- down_weight: bfloat16 [28672, 8192], P('hidden', 'mp'), may hold values from -0.03125 to 0.03125
Outputs:
- grad_input: bfloat16 [512, 8192], P('hidden', 'mp')
- sal_gate: bfloat16 [8192, 28672], P('mp', 'hidden')
- sal_up: bfloat16 [8192, 28672], P('mp', 'hidden')
- sal_down: bfloat16 [28672, 8192], P('hidden', 'mp')
The draws below stay inside these ranges and needn't reach their ends.
All inputs are finite; a program needn't handle non-finite values.
Results may differ from the reference program's by a relative error of at most 0.0049.
Values may be sent and summed in bfloat16 or wider, within the bound.
A program may use at most 128 MiB of HBM per device.

```python
import jax
import jax.numpy as jnp
from jax import lax

D = 8192
FF = 28672
TOKENS = 512


def steps_of(key, extent, cuts, smallest, largest):
    gain, own = 1.0, jax.random.fold_in(key, 6)
    for dim, parts in cuts:
        steps = jnp.exp(jax.random.uniform(jax.random.fold_in(own, dim), (parts,), jnp.float32, smallest / len(cuts), largest / len(cuts)))
        gain = gain * jnp.repeat(steps, extent[dim] // parts).reshape([-1 if axis == dim else 1 for axis in range(len(extent))])
    return gain


def bell_draw(stream_key, shape, spread, bound, pieces=(), held_as=jnp.bfloat16):
    values = jax.random.normal(stream_key, shape, jnp.float32) * spread
    if len(pieces) > 0:
        values = steps_of(stream_key, shape, pieces, -0.22, 0.18) * values
    return jnp.clip(values, min=-bound, max=bound).astype(held_as)


def setup_inputs(seed: int = 0) -> dict:
    splits = jax.random.split(jax.random.key(seed), 6)
    tokens = bell_draw(splits[0], (TOKENS, D), 1.0, 6.0, ((0, 16), (1, 16)))
    grad_output = bell_draw(splits[1], (TOKENS, D), 1.0, 6.0, ((0, 16), (1, 16)))
    gate_weight = bell_draw(splits[2], (D, FF), D ** -0.5, 0.0625, ((0, 16), (1, 16)))
    up_weight = bell_draw(splits[3], (D, FF), D ** -0.5, 0.0625, ((0, 16), (1, 16)))
    down_weight = bell_draw(splits[4], (FF, D), FF ** -0.5, 0.03125, ((0, 16), (1, 16)))
    return dict(tokens=tokens, grad_output=grad_output, gate_weight=gate_weight, up_weight=up_weight, down_weight=down_weight)


def reference(tokens, grad_output, gate_weight, up_weight, down_weight):
    gate = jnp.dot(tokens, gate_weight, preferred_element_type=jnp.float32)
    up = jnp.dot(tokens, up_weight, preferred_element_type=jnp.float32)
    grad_hidden = lax.dot_general(grad_output, down_weight, (((1,), (1,)), ((), ())), preferred_element_type=jnp.float32)
    sig = jax.nn.sigmoid(gate)
    silu_gate = gate * sig
    hidden = (silu_gate * up).astype(jnp.bfloat16)
    grad_gate = (grad_hidden * up * sig * (1.0 + gate * (1.0 - sig))).astype(jnp.bfloat16)
    grad_up = (grad_hidden * silu_gate).astype(jnp.bfloat16)
    down_grad = lax.dot_general(hidden, grad_output, (((0,), (0,)), ((), ())), preferred_element_type=jnp.float32)
    sal_down = jnp.abs(down_weight.astype(jnp.float32) * down_grad).astype(jnp.bfloat16)
    gate_grad = lax.dot_general(tokens, grad_gate, (((0,), (0,)), ((), ())), preferred_element_type=jnp.float32)
    sal_gate = jnp.abs(gate_weight.astype(jnp.float32) * gate_grad).astype(jnp.bfloat16)
    up_grad = lax.dot_general(tokens, grad_up, (((0,), (0,)), ((), ())), preferred_element_type=jnp.float32)
    sal_up = jnp.abs(up_weight.astype(jnp.float32) * up_grad).astype(jnp.bfloat16)
    back_gate = lax.dot_general(grad_gate, gate_weight, (((1,), (1,)), ((), ())), preferred_element_type=jnp.float32)
    back_up = lax.dot_general(grad_up, up_weight, (((1,), (1,)), ((), ())), preferred_element_type=jnp.float32)
    grad_input = (back_gate + back_up).astype(jnp.bfloat16)
    return grad_input, sal_gate, sal_up, sal_down
```

```python
import jax
import jax.numpy as jnp
from jax import lax
from jax.experimental import pallas as pl
from jax.experimental.pallas import tpu as pltpu
from jax.sharding import PartitionSpec as P

MESH = pl.DeviceIdType.MESH
F32 = jnp.float32
BF16 = jnp.bfloat16
HALF = 896
PHASES = ((0, 512), (512, 384))
BLOCK = 64


def encode(value):
    return (value * jnp.abs(value)).astype(BF16)


def decode(sent):
    square = sent.astype(F32)
    size = jnp.abs(square)
    root = size * lax.rsqrt(jnp.maximum(size, 1e-36))
    return jnp.where(square < 0, -root, root)


def dot_nt(left, right):
    return lax.dot_general(left, right, (((1,), (1,)), ((), ())), preferred_element_type=F32)


def dot_tn(left, right):
    return lax.dot_general(left, right, (((0,), (0,)), ((), ())), preferred_element_type=F32)


def kernel(
    tok_ref, go_ref, wg_ref, wu_ref, wd_ref,
    gi_ref, sg_ref, su_ref, sd_ref,
    act_in, act_px, w_gu, w_d, px_gu, px_d,
    rs_send0, rs_send1, rs_recv0, rs_recv1, first0, first1,
    all0, all1, gi_send, gi_recv, out_gu, out_d,
    load_sem, px_send, px_recv, tok_send, tok_recv, share_send, share_recv,
    rs_ssem, rs_rsem, ag_ssem, ag_rsem, pair_send, pair_recv, gi_ssem, gi_rsem, out_sem,
):
    mp, hid = lax.axis_index("mp"), lax.axis_index("hidden")
    z, core = mp // 2, mp % 2
    y, x = hid // 4, hid % 4
    rs_send, rs_recv, first, gathered = (rs_send0, rs_send1), (rs_recv0, rs_recv1), (first0, first1), (all0, all1)

    def remote(src, dst, ssem, rsem, device):
        return pltpu.make_async_remote_copy(
            src_ref=src, dst_ref=dst, send_sem=ssem, recv_sem=rsem, device_id=device, device_id_type=MESH
        )

    def ring(way):
        return (lax.rem(z + 1 + 6 * way, 8) * 2 + core, hid)

    partner = (z * 2 + (1 - core), hid)

    def in_plane(j):
        return (mp, lax.rem(hid + j, 16))

    def along(a, axis, step):
        if (a + axis) % 2 == 0:
            return (mp, y * 4 + lax.rem(x + step, 4))
        return (mp, lax.rem(y + step, 4) * 4 + x)

    own_col = pl.multiple_of(core * HALF, 128)
    other_col = pl.multiple_of((1 - core) * HALF, 128)

    loads = []

    def load(src, dst):
        copy = pltpu.make_async_copy(src, dst, load_sem.at[len(loads)])
        copy.start()
        loads.append(copy)

    load(tok_ref, act_in.at[0, y, x])
    load(go_ref, act_in.at[1, y, x])
    for half, col in ((0, own_col), (1, other_col)):
        load(wg_ref.at[:, pl.ds(col, HALF)], w_gu.at[half, 0])
        load(wu_ref.at[:, pl.ds(col, HALF)], w_gu.at[half, 1])
        load(wd_ref.at[pl.ds(col, HALF), :], w_d.at[half])

    barrier = pltpu.get_barrier_semaphore()
    for j in range(1, 16):
        pl.semaphore_signal(barrier, inc=1, device_id=in_plane(j), device_id_type=MESH)
    for device in (ring(0), ring(1), partner):
        pl.semaphore_signal(barrier, inc=1, device_id=device, device_id_type=MESH)
    pl.semaphore_wait(barrier, 18)

    sources = (tok_ref, go_ref)
    line_copies = []
    for a in range(2):
        for j, step in enumerate((1, 3, 2)):
            copy = remote(
                sources[a], act_in.at[a, y, x], tok_send.at[a, j], tok_recv.at[a, j], along(a, 0, step)
            )
            copy.start()
            line_copies.append(copy)
    px_copies = []
    for i, (src, dst) in enumerate((
        (wg_ref.at[:, pl.ds(other_col, HALF)], px_gu.at[0]),
        (wu_ref.at[:, pl.ds(other_col, HALF)], px_gu.at[1]),
        (wd_ref.at[pl.ds(other_col, HALF), :], px_d),
    )):
        copy = remote(src, dst, px_send.at[i], px_recv.at[i], partner)
        copy.start()
        px_copies.append(copy)

    def line(a, step, part=None):
        if a == 0:
            at = lax.rem(y + step, 4)
            return act_in.at[0, at] if part is None else act_in.at[0, at, 2 * part : 2 * part + 2]
        at = lax.rem(x + step, 4)
        return act_in.at[1, :, at] if part is None else act_in.at[1, 2 * part : 2 * part + 2, at]

    def line_px(a, step):
        if a == 0:
            return act_px.at[0, lax.rem(y + step, 4)]
        return act_px.at[1, :, lax.rem(x + step, 4)]

    def share(a, step):
        copy = remote(
            line(a, step), line_px(a, step), share_send.at[a, step], share_recv.at[a, step], partner
        )
        copy.start()
        share_copies.append(copy)

    share_copies = []
    wide = {}
    for a in range(2):
        loads[a].wait()
        for j in range(3):
            line_copies[3 * a + j].wait_recv()
        for way, part in ((0, 0), (1, 1), (0, 1), (1, 0)):
            i = 3 + 2 * way + part
            copy = remote(
                line(a, 0, part), line(a, 0, part), tok_send.at[a, i], tok_recv.at[a, i],
                along(a, 1, 1 if way == 0 else 3),
            )
            copy.start()
            wide[a, way, part] = copy
        share(a, 0)
    far = {}
    for a in range(2):
        for way in range(2):
            wide[a, way, way].wait_recv()
            step = 3 if way == 0 else 1
            i = 7 + way
            copy = remote(
                line(a, step, way), line(a, step, way), tok_send.at[a, i], tok_recv.at[a, i],
                along(a, 1, 1 if way == 0 else 3),
            )
            copy.start()
            far[a, way] = copy
    for a in range(2):
        for way in range(2):
            wide[a, way, 1 - way].wait_recv()
            share(a, 3 if way == 0 else 1)
    for copy in loads[2:]:
        copy.wait()
    for p in range(2):
        width = PHASES[p][1]
        for m in range(3):
            rs_recv[p][0, 0, m, 32:64, :] = jnp.zeros((32, width), BF16)
            rs_recv[p][1, 0, m, 0:32, :] = jnp.zeros((32, width), BF16)
    for copy in px_copies:
        copy.wait_recv()
    for a in range(2):
        far[a, 0].wait_recv()
        far[a, 1].wait_recv()
        share(a, 2)
    for copy in share_copies:
        copy.wait_recv()

    def partial(p, m, d):
        c0, width = PHASES[p]
        a = 1 if m == 2 else 0
        rows = (d // 2, pl.ds(lax.rem(d, 2) * 2, 2))
        mine = act_in[a, rows[0], rows[1]].reshape(BLOCK, 512)
        theirs = act_px[a, rows[0], rows[1]].reshape(BLOCK, 512)
        if m == 2:
            return dot_nt(mine, w_d[0, c0 : c0 + width, :]) + dot_nt(theirs, px_d[c0 : c0 + width, :])
        return jnp.dot(mine, w_gu[0, m, :, c0 : c0 + width], preferred_element_type=F32) + jnp.dot(
            theirs, px_gu[m, :, c0 : c0 + width], preferred_element_type=F32
        )

    def first_copy(p, way, m):
        rows = slice(32 * way, 32 * way + 32)
        return remote(
            first[p].at[m, rows], rs_recv[p].at[way, 0, m, rows],
            rs_ssem.at[p, way, 0, m], rs_rsem.at[p, way, 0, m], ring(way),
        )

    def next_copy(p, way, step, m):
        return remote(
            rs_send[p].at[way, step - 1, m], rs_recv[p].at[way, step, m],
            rs_ssem.at[p, way, step, m], rs_rsem.at[p, way, step, m], ring(way),
        )

    def reduce_first(p):
        for m in range(3):
            first[p][m] = encode(partial(p, m, lax.rem(z + 4, 8)))
            for way in range(2):
                first_copy(p, way, m).start()

    def reduce_rest(p):
        def body(t, _):
            way, step = lax.rem(t, 2), t // 2 + 1
            distance = 4 - step
            d = lax.rem(z + distance + way * (8 - 2 * distance), 8)
            for m in range(3):
                mine = partial(p, m, d)

                @pl.when(step == 1)
                def _():
                    @pl.when(way == 0)
                    def _():
                        first_copy(p, 0, m).wait_recv()

                    @pl.when(way == 1)
                    def _():
                        first_copy(p, 1, m).wait_recv()

                @pl.when(step > 1)
                def _():
                    next_copy(p, way, step - 1, m).wait_recv()

                rs_send[p][way, step - 1, m] = encode(mine + decode(rs_recv[p][way, step - 1, m]))
                next_copy(p, way, step, m).start()
            return 0

        lax.fori_loop(0, 6, body, 0)

    own_rows = pl.ds(pl.multiple_of(z * BLOCK, BLOCK), BLOCK)

    def activate(p):
        sums = []
        for m in range(3):
            mine = partial(p, m, z)
            for way in range(2):
                next_copy(p, way, 3, m).wait_recv()
            sums.append(mine + decode(rs_recv[p][0, 3, m]) + decode(rs_recv[p][1, 3, m]))
        gate, up, grad_hidden = sums
        sig = jax.nn.sigmoid(gate)
        silu_gate = gate * sig
        gathered[p][0, 0, own_rows] = (silu_gate * up).astype(BF16)
        gathered[p][0, 1, own_rows] = (grad_hidden * up * sig * (1.0 + gate * (1.0 - sig))).astype(BF16)
        gathered[p][0, 2, own_rows] = (grad_hidden * silu_gate).astype(BF16)

    def block_of(way, step):
        return lax.rem(z + (8 - step if way == 0 else step), 8)

    def spread_copy(p, way, step, m):
        start = block_of(way, step) * BLOCK
        count = BLOCK
        if step == 3:
            start, count = start + 32 * way, 32
        rows = pl.ds(pl.multiple_of(start, 32), count)
        ref = gathered[p].at[0, m, rows]
        return remote(ref, ref, ag_ssem.at[p, way, step, m], ag_rsem.at[p, way, step, m], ring(way))

    def pair_copy(p, k):
        d = lax.rem(z + (0, 7, 6, 5, 1, 2, 3, 4)[k], 8)
        rows = pl.ds(pl.multiple_of(d * BLOCK, BLOCK), BLOCK)
        return remote(
            gathered[p].at[0, :, rows], gathered[p].at[1, :, rows], pair_send.at[p, k], pair_recv.at[p, k], partner
        )

    def spread_first(p):
        for m in range(3):
            for way in range(2):
                spread_copy(p, way, 0, m).start()
        pair_copy(p, 0).start()

    def spread_next(p, step):
        for m in range(3):
            for way in range(2):
                spread_copy(p, way, step - 1, m).wait_recv()
                spread_copy(p, way, step, m).start()
        pair_copy(p, step).start()
        pair_copy(p, 3 + step).start()

    def spread_last(p):
        for m in range(3):
            for way in range(2):
                spread_copy(p, way, 3, m).wait_recv()
        pair_copy(p, 7).start()

    def grad_in(half, mat, p):
        c0, width = PHASES[p]
        cols = slice(c0, c0 + width)
        right = gathered[p][half, 1 + mat]
        tokens = act_in[0].reshape(512, 512)
        grads = dot_tn(tokens, right)
        out_gu[half, mat, :, cols] = jnp.abs(w_gu[half, mat, :, cols].astype(F32) * grads).astype(BF16)

    def saliency_gu(p, mat):
        def body(half, _):
            grad_in(half, mat, p)
            return 0

        lax.fori_loop(0, 2, body, 0)

    def saliency_d(p):
        c0, width = PHASES[p]

        def body(half, _):
            grads = dot_tn(gathered[p][half, 0], act_in[1].reshape(512, 512))
            rows = slice(c0, c0 + width)
            out_d[half, rows, :] = jnp.abs(w_d[half, rows, :].astype(F32) * grads).astype(BF16)
            return 0

        lax.fori_loop(0, 2, body, 0)

    outs = []

    def store(p, m):
        c0, width = PHASES[p]
        for half, base in ((0, own_col), (1, other_col)):
            at = pl.ds(pl.multiple_of(base + c0, 128), width)
            if m == 2:
                src, dst = out_d.at[half, c0 : c0 + width, :], sd_ref.at[at, :]
            else:
                src, dst = out_gu.at[half, m, :, c0 : c0 + width], (sg_ref, su_ref)[m].at[:, at]
            copy = pltpu.make_async_copy(src, dst, out_sem.at[p, m, half])
            copy.start()
            outs.append(copy)

    def gi_copy(d, part):
        dest = 2 * d + part
        return remote(
            gi_send.at[d, 32 * part : 32 * part + 32], gi_recv.at[hid],
            gi_ssem.at[d, part], gi_rsem.at[hid], (mp, dest),
        )

    def input_grad(d):
        rows = pl.ds(pl.multiple_of(d * BLOCK, BLOCK), BLOCK)
        total = jnp.zeros((BLOCK, 512), F32)
        for p in range(2):
            c0, width = PHASES[p]
            for half in range(2):
                for mat in range(2):
                    total += dot_nt(gathered[p][half, 1 + mat, rows], w_gu[half, mat, :, c0 : c0 + width])
        gi_send[d] = encode(total)
        for part in range(2):
            @pl.when(hid != 2 * d + part)
            def _():
                gi_copy(d, part).start()

    reduce_first(0)
    reduce_rest(0)
    reduce_first(1)
    activate(0)
    reduce_rest(1)
    spread_first(0)
    activate(1)
    for step in (1, 2, 3):
        spread_next(0, step)
    spread_first(1)
    spread_last(0)
    spread_next(1, 1)
    for k in range(8):
        pair_copy(0, k).wait_recv()
    saliency_gu(0, 0)
    store(0, 0)
    spread_next(1, 2)
    saliency_gu(0, 1)
    store(0, 1)
    spread_next(1, 3)
    saliency_d(0)
    store(0, 2)

    for k in range(7):
        pair_copy(1, k).wait_recv()

    def near(j, _):
        input_grad(lax.rem(z + 5 + j, 8))
        return 0

    lax.fori_loop(0, 7, near, 0)
    spread_last(1)
    pair_copy(1, 7).wait_recv()
    input_grad(lax.rem(z + 4, 8))
    for m in range(2):
        saliency_gu(1, m)
        store(1, m)
    saliency_d(1)
    store(1, 2)

    total = decode(gi_send[hid // 2, pl.ds(pl.multiple_of(lax.rem(hid, 2) * 32, 32), 32)])
    for j in range(1, 16):
        slot = lax.rem(hid + j, 16)
        remote(
            gi_send.at[0, 0:32], gi_recv.at[slot], gi_ssem.at[0, 0], gi_rsem.at[slot], in_plane(j)
        ).wait_recv()
        total += decode(gi_recv[slot])
    gi_ref[...] = total.astype(BF16)

    for copy in line_copies + px_copies + share_copies + list(wide.values()) + list(far.values()):
        copy.wait_send()
    for p in range(2):
        for way in range(2):
            for m in range(3):
                first_copy(p, way, m).wait_send()
                for step in (1, 2, 3):
                    next_copy(p, way, step, m).wait_send()
                for step in range(4):
                    spread_copy(p, way, step, m).wait_send()
        for k in range(8):
            pair_copy(p, k).wait_send()

    def sent(d, _):
        for part in range(2):
            @pl.when(hid != 2 * d + part)
            def _():
                gi_copy(d, part).wait_send()
        return 0

    lax.fori_loop(0, 8, sent, 0)
    for copy in outs:
        copy.wait()


def local(tokens, grad_output, gate_weight, up_weight, down_weight):
    anywhere = pl.BlockSpec(memory_space=pl.ANY)
    dma = pltpu.SemaphoreType.DMA
    sizes = [width for _, width in PHASES]
    return pl.pallas_call(
        kernel,
        out_shape=(
            jax.ShapeDtypeStruct((32, 512), BF16),
            jax.ShapeDtypeStruct((512, 1792), BF16),
            jax.ShapeDtypeStruct((512, 1792), BF16),
            jax.ShapeDtypeStruct((1792, 512), BF16),
        ),
        in_specs=[anywhere] * 5,
        out_specs=(pl.BlockSpec(memory_space=pltpu.VMEM), anywhere, anywhere, anywhere),
        scratch_shapes=[
            pltpu.VMEM((2, 4, 4, 32, 512), BF16),
            pltpu.VMEM((2, 4, 4, 32, 512), BF16),
            pltpu.VMEM((2, 2, 512, HALF), BF16),
            pltpu.VMEM((2, HALF, 512), BF16),
            pltpu.VMEM((2, 512, HALF), BF16),
            pltpu.VMEM((HALF, 512), BF16),
            *[pltpu.VMEM((2, 3, 3, BLOCK, width), BF16) for width in sizes],
            *[pltpu.VMEM((2, 4, 3, BLOCK, width), BF16) for width in sizes],
            *[pltpu.VMEM((3, BLOCK, width), BF16) for width in sizes],
            *[pltpu.VMEM((2, 3, 512, width), BF16) for width in sizes],
            pltpu.VMEM((8, BLOCK, 512), BF16),
            pltpu.VMEM((16, 32, 512), BF16),
            pltpu.VMEM((2, 2, 512, HALF), BF16),
            pltpu.VMEM((2, HALF, 512), BF16),
            dma((8,)),
            dma((3,)),
            dma((3,)),
            dma((2, 9)),
            dma((2, 9)),
            dma((2, 4)),
            dma((2, 4)),
            dma((2, 2, 4, 3)),
            dma((2, 2, 4, 3)),
            dma((2, 2, 4, 3)),
            dma((2, 2, 4, 3)),
            dma((2, 8)),
            dma((2, 8)),
            dma((8, 2)),
            dma((16,)),
            dma((2, 3, 2)),
        ],
        compiler_params=pltpu.CompilerParams(
            collective_id=0, has_side_effects=True, vmem_limit_bytes=56 * 2**20
        ),
        cost_estimate=pl.CostEstimate(flops=7_516_192_768, bytes_accessed=11_010_048, transcendentals=2_000_000),
    )(tokens, grad_output, gate_weight, up_weight, down_weight)


def solution(mesh):
    return jax.shard_map(
        local,
        mesh=mesh,
        in_specs=(
            P("hidden", "mp"),
            P("hidden", "mp"),
            P("mp", "hidden"),
            P("mp", "hidden"),
            P("hidden", "mp"),
        ),
        out_specs=(P("hidden", "mp"), P("mp", "hidden"), P("mp", "hidden"), P("hidden", "mp")),
        check_vma=False,
    )
```

```python
import jax
import jax.numpy as jnp
from jax import lax
from jax.experimental import pallas as pl
from jax.experimental.pallas import tpu as pltpu
from jax.sharding import PartitionSpec as P

MESH = pl.DeviceIdType.MESH
F32 = jnp.float32
BF16 = jnp.bfloat16
HALF = 896
PHASES = ((0, 512), (512, 384))
BLOCK = 64


def encode(value):
    return (value * jnp.abs(value)).astype(BF16)


def decode(sent):
    square = sent.astype(F32)
    size = jnp.abs(square)
    root = size * lax.rsqrt(jnp.maximum(size, 1e-36))
    return jnp.where(square < 0, -root, root)


def dot_nt(left, right):
    return lax.dot_general(left, right, (((1,), (1,)), ((), ())), preferred_element_type=F32)


def dot_tn(left, right):
    return lax.dot_general(left, right, (((0,), (0,)), ((), ())), preferred_element_type=F32)


def kernel(
    tok_ref, go_ref, wg_ref, wu_ref, wd_ref,
    gi_ref, out_gu, out_d,
    act_in, act_px, w_gu, w_d, px_gu, px_d,
    rs_send0, rs_send1, rs_recv0, rs_recv1, first0, first1, mine0, mine1,
    all0, all1, gi_send, gi_recv,
    load_sem, px_send, px_recv, tok_send, tok_recv, share_send, share_recv,
    rs_ssem, rs_rsem, ag_ssem, ag_rsem, pair_send, pair_recv, gi_ssem, gi_rsem,
):
    mp, hid = lax.axis_index("mp"), lax.axis_index("hidden")
    z, core = mp // 2, mp % 2
    y, x = hid // 4, hid % 4
    rs_send, rs_recv, first = (rs_send0, rs_send1), (rs_recv0, rs_recv1), (first0, first1)
    own, gathered = (mine0, mine1), (all0, all1)

    def remote(src, dst, ssem, rsem, device):
        return pltpu.make_async_remote_copy(
            src_ref=src, dst_ref=dst, send_sem=ssem, recv_sem=rsem, device_id=device, device_id_type=MESH
        )

    def ring(way):
        return (lax.rem(z + 1 + 6 * way, 8) * 2 + core, hid)

    partner = (z * 2 + (1 - core), hid)

    def in_plane(j):
        return (mp, lax.rem(hid + j, 16))

    def along(f, axis, step):
        if (f + axis) % 2 == 0:
            return (mp, y * 4 + lax.rem(x + step, 4))
        return (mp, lax.rem(y + step, 4) * 4 + x)

    own_col = pl.multiple_of(core * HALF, 128)
    other_col = pl.multiple_of((1 - core) * HALF, 128)

    loads = []

    def load(src, dst):
        copy = pltpu.make_async_copy(src, dst, load_sem.at[len(loads)])
        copy.start()
        loads.append(copy)

    load(tok_ref, act_in.at[0, y, x])
    load(go_ref, act_in.at[1, y, x])
    for half, col in ((0, own_col), (1, other_col)):
        load(wg_ref.at[:, pl.ds(col, HALF)], w_gu.at[half, 0])
        load(wu_ref.at[:, pl.ds(col, HALF)], w_gu.at[half, 1])
        load(wd_ref.at[pl.ds(col, HALF), :], w_d.at[half])

    barrier = pltpu.get_barrier_semaphore()
    for j in range(1, 16):
        pl.semaphore_signal(barrier, inc=1, device_id=in_plane(j), device_id_type=MESH)
    for device in (ring(0), ring(1), partner):
        pl.semaphore_signal(barrier, inc=1, device_id=device, device_id_type=MESH)
    pl.semaphore_wait(barrier, 18)

    for p in range(2):
        width = PHASES[p][1]
        for m in range(3):
            rs_recv[p][0, 0, m, 32:64, :] = jnp.zeros((32, width), BF16)
            rs_recv[p][1, 0, m, 0:32, :] = jnp.zeros((32, width), BF16)

    sources = (tok_ref, go_ref)
    columns = (slice(0, 256), slice(256, 512))
    copies = []

    def begin(copy):
        copy.start()
        copies.append(copy)
        return copy

    near = {}
    for a in range(2):
        for f in range(2):
            for j, step in enumerate((1, 3, 2)):
                near[a, f, j] = begin(remote(
                    sources[a].at[:, columns[f]], act_in.at[a, y, x, :, columns[f]],
                    tok_send.at[a, f, j], tok_recv.at[a, f, j], along(f, 0, step),
                ))
    px_copies = []
    for i, (src, dst) in enumerate((
        (wg_ref.at[:, pl.ds(other_col, HALF)], px_gu.at[0]),
        (wu_ref.at[:, pl.ds(other_col, HALF)], px_gu.at[1]),
        (wd_ref.at[pl.ds(other_col, HALF), :], px_d),
    )):
        px_copies.append(begin(remote(src, dst, px_send.at[i], px_recv.at[i], partner)))

    def line(ref, a, f, step, part=None):
        span = slice(0, 4) if part is None else slice(2 * part, 2 * part + 2)
        if f == 0:
            return ref.at[a, lax.rem(y + step, 4), span, :, columns[0]]
        return ref.at[a, span, lax.rem(x + step, 4), :, columns[1]]

    shares = {}

    def share(a, f, step):
        shares[a, f, step] = begin(remote(
            line(act_in, a, f, step), line(act_px, a, f, step),
            share_send.at[a, f, step], share_recv.at[a, f, step], partner,
        ))

    wide, far = {}, {}

    def send_lines(a):
        loads[a].wait()
        for f in range(2):
            for j in range(3):
                near[a, f, j].wait_recv()
        for way, part in ((0, 0), (1, 1), (0, 1), (1, 0)):
            for f in range(2):
                i = 3 + 2 * way + part
                ref = line(act_in, a, f, 0, part)
                wide[a, f, way, part] = begin(remote(
                    ref, ref, tok_send.at[a, f, i], tok_recv.at[a, f, i], along(f, 1, 1 if way == 0 else 3)
                ))
        for f in range(2):
            share(a, f, 0)

    def pass_on(a):
        for way in range(2):
            for f in range(2):
                wide[a, f, way, way].wait_recv()
                ref = line(act_in, a, f, 3 if way == 0 else 1, way)
                far[a, f, way] = begin(remote(
                    ref, ref, tok_send.at[a, f, 7 + way], tok_recv.at[a, f, 7 + way],
                    along(f, 1, 1 if way == 0 else 3),
                ))
        for way in range(2):
            for f in range(2):
                wide[a, f, way, 1 - way].wait_recv()
                share(a, f, 3 if way == 0 else 1)

    def finish(a):
        for f in range(2):
            far[a, f, 0].wait_recv()
            far[a, f, 1].wait_recv()
            share(a, f, 2)
        for f in range(2):
            for step in range(4):
                shares[a, f, step].wait_recv()

    send_lines(0)
    pass_on(0)
    send_lines(1)
    for copy in loads[2:]:
        copy.wait()
    for copy in px_copies:
        copy.wait_recv()
    finish(0)

    def block(ref, a, d):
        return ref[a, d // 2, pl.ds(lax.rem(d, 2) * 2, 2)].reshape(BLOCK, 512)

    def partial(p, m, *ds):
        c0, width = PHASES[p]
        a = 1 if m == 2 else 0
        ours, theirs = [
            jnp.concatenate([block(ref, a, d) for d in ds]) if len(ds) > 1 else block(ref, a, ds[0])
            for ref in (act_in, act_px)
        ]
        if m == 2:
            return dot_nt(ours, w_d[0, c0 : c0 + width, :]) + dot_nt(theirs, px_d[c0 : c0 + width, :])
        return jnp.dot(ours, w_gu[0, m, :, c0 : c0 + width], preferred_element_type=F32) + jnp.dot(
            theirs, px_gu[m, :, c0 : c0 + width], preferred_element_type=F32
        )

    def first_copy(p, way, m):
        rows = slice(32 * way, 32 * way + 32)
        return remote(
            first[p].at[m, rows], rs_recv[p].at[way, 0, m, rows],
            rs_ssem.at[p, way, 0, m], rs_rsem.at[p, way, 0, m], ring(way),
        )

    def next_copy(p, way, step, m):
        return remote(
            rs_send[p].at[way, step - 1, m], rs_recv[p].at[way, step, m],
            rs_ssem.at[p, way, step, m], rs_rsem.at[p, way, step, m], ring(way),
        )

    pieces = ((0, 0), (0, 1), (1, 0), (1, 1), (0, 2), (1, 2))

    def reduce_first(p, m):
        first[p][m] = encode(partial(p, m, lax.rem(z + 4, 8)))
        for way in range(2):
            first_copy(p, way, m).start()

    def reduce_step(step, _):
        for p, m in pieces:
            both = partial(p, m, lax.rem(z + 4 - step, 8), lax.rem(z + 4 + step, 8))
            for way in range(2):
                @pl.when(step == 1)
                def _():
                    first_copy(p, way, m).wait_recv()

                @pl.when(step > 1)
                def _():
                    next_copy(p, way, step - 1, m).wait_recv()

                mine = both[BLOCK * way : BLOCK * way + BLOCK]
                rs_send[p][way, step - 1, m] = encode(mine + decode(rs_recv[p][way, step - 1, m]))
                next_copy(p, way, step, m).start()
        return 0

    own_rows = pl.ds(pl.multiple_of(z * BLOCK, BLOCK), BLOCK)

    def activate(p):
        sums = []
        for m in range(3):
            for way in range(2):
                next_copy(p, way, 3, m).wait_recv()
            sums.append(own[p][m] + decode(rs_recv[p][0, 3, m]) + decode(rs_recv[p][1, 3, m]))
        gate, up, grad_hidden = sums
        sig = jax.nn.sigmoid(gate)
        silu_gate = gate * sig
        gathered[p][0, 0, own_rows] = (silu_gate * up).astype(BF16)
        gathered[p][0, 1, own_rows] = (grad_hidden * up * sig * (1.0 + gate * (1.0 - sig))).astype(BF16)
        gathered[p][0, 2, own_rows] = (grad_hidden * silu_gate).astype(BF16)

    def block_of(way, step):
        return lax.rem(z + (8 - step if way == 0 else step), 8)

    def spread_copy(p, way, step, m):
        start = block_of(way, step) * BLOCK
        count = BLOCK
        if step == 3:
            start, count = start + 32 * way, 32
        rows = pl.ds(pl.multiple_of(start, 32), count)
        ref = gathered[p].at[0, m, rows]
        return remote(ref, ref, ag_ssem.at[p, way, step, m], ag_rsem.at[p, way, step, m], ring(way))

    def pair_copy(p, k):
        d = lax.rem(z + (0, 7, 6, 5, 1, 2, 3, 4)[k], 8)
        rows = pl.ds(pl.multiple_of(d * BLOCK, BLOCK), BLOCK)
        return remote(
            gathered[p].at[0, :, rows], gathered[p].at[1, :, rows], pair_send.at[p, k], pair_recv.at[p, k], partner
        )

    def spread_first(p):
        for m in range(3):
            for way in range(2):
                spread_copy(p, way, 0, m).start()
        pair_copy(p, 0).start()

    def spread_next(p, step):
        for m in range(3):
            for way in range(2):
                spread_copy(p, way, step - 1, m).wait_recv()
                spread_copy(p, way, step, m).start()
        pair_copy(p, step).start()
        pair_copy(p, 3 + step).start()

    def spread_last(p):
        for m in range(3):
            for way in range(2):
                spread_copy(p, way, 3, m).wait_recv()
        pair_copy(p, 7).start()

    def grad_in(half, mat, p):
        c0, width = PHASES[p]
        cols = slice(c0, c0 + width)
        right = gathered[p][half, 1 + mat]
        tokens = act_in[0].reshape(512, 512)
        grads = dot_tn(tokens, right)
        out_gu[half, mat, :, cols] = jnp.abs(w_gu[half, mat, :, cols].astype(F32) * grads).astype(BF16)

    def saliency_gu(p, mat):
        def body(half, _):
            grad_in(half, mat, p)
            return 0

        lax.fori_loop(0, 2, body, 0)

    def saliency_d(p):
        c0, width = PHASES[p]

        def body(half, _):
            grads = dot_tn(gathered[p][half, 0], act_in[1].reshape(512, 512))
            rows = slice(c0, c0 + width)
            out_d[half, rows, :] = jnp.abs(w_d[half, rows, :].astype(F32) * grads).astype(BF16)
            return 0

        lax.fori_loop(0, 2, body, 0)

    def gi_copy(d, part):
        dest = 2 * d + part
        return remote(
            gi_send.at[d, 32 * part : 32 * part + 32], gi_recv.at[hid],
            gi_ssem.at[d, part], gi_rsem.at[hid], (mp, dest),
        )

    def input_grad(*ds):
        total = jnp.zeros((BLOCK * len(ds), 512), F32)
        for p in range(2):
            c0, width = PHASES[p]
            for half in range(2):
                for mat in range(2):
                    left = [
                        gathered[p][half, 1 + mat, pl.ds(pl.multiple_of(d * BLOCK, BLOCK), BLOCK)] for d in ds
                    ]
                    left = jnp.concatenate(left) if len(ds) > 1 else left[0]
                    total += dot_nt(left, w_gu[half, mat, :, c0 : c0 + width])
        for i, d in enumerate(ds):
            gi_send[d] = encode(total[BLOCK * i : BLOCK * i + BLOCK])
            for part in range(2):
                @pl.when(hid != 2 * d + part)
                def _():
                    gi_copy(d, part).start()

    for p, m in pieces[:4]:
        reduce_first(p, m)
    pass_on(1)
    finish(1)
    for p, m in pieces[4:]:
        reduce_first(p, m)
    lax.fori_loop(1, 4, reduce_step, 0)
    for p, m in pieces:
        own[p][m] = partial(p, m, z)
    for p in range(2):
        activate(p)
        spread_first(p)
    for step in (1, 2, 3):
        for p in range(2):
            spread_next(p, step)
        if step == 1:
            pair_copy(0, 0).wait_recv()
            pair_copy(1, 0).wait_recv()
            input_grad(z)
        else:
            for p in range(2):
                pair_copy(p, step - 1).wait_recv()
                pair_copy(p, step + 2).wait_recv()
            input_grad(lax.rem(z + 9 - step, 8), lax.rem(z + step - 1, 8))
    for p in range(2):
        pair_copy(p, 3).wait_recv()
        pair_copy(p, 6).wait_recv()
    input_grad(lax.rem(z + 5, 8), lax.rem(z + 3, 8))
    for p in range(2):
        spread_last(p)
    for p in range(2):
        pair_copy(p, 7).wait_recv()
    input_grad(lax.rem(z + 4, 8))
    for p in range(2):
        for mat in range(2):
            saliency_gu(p, mat)
        saliency_d(p)

    total = decode(gi_send[hid // 2, pl.ds(pl.multiple_of(lax.rem(hid, 2) * 32, 32), 32)])
    for j in range(1, 16):
        slot = lax.rem(hid + j, 16)
        remote(
            gi_send.at[0, 0:32], gi_recv.at[slot], gi_ssem.at[0, 0], gi_rsem.at[slot], in_plane(j)
        ).wait_recv()
        total += decode(gi_recv[slot])
    gi_ref[...] = total.astype(BF16)

    for copy in copies:
        copy.wait_send()
    for p in range(2):
        for way in range(2):
            for m in range(3):
                first_copy(p, way, m).wait_send()
                for step in (1, 2, 3):
                    next_copy(p, way, step, m).wait_send()
                for step in range(4):
                    spread_copy(p, way, step, m).wait_send()
        for k in range(8):
            pair_copy(p, k).wait_send()

    def sent(d, _):
        for part in range(2):
            @pl.when(hid != 2 * d + part)
            def _():
                gi_copy(d, part).wait_send()
        return 0

    lax.fori_loop(0, 8, sent, 0)


def write_out(gi_in, gu_in, d_in, gi_ref, sg_ref, su_ref, sd_ref, sem):
    core = lax.rem(lax.axis_index("mp"), 2)
    copies = [pltpu.make_async_copy(gi_in, gi_ref, sem.at[6])]
    for half in range(2):
        at = pl.ds(pl.multiple_of((core + half * (1 - 2 * core)) * HALF, 128), HALF)
        for m, (src, dst) in enumerate((
            (gu_in.at[half, 0], sg_ref.at[:, at]),
            (gu_in.at[half, 1], su_ref.at[:, at]),
            (d_in.at[half], sd_ref.at[at, :]),
        )):
            copies.append(pltpu.make_async_copy(src, dst, sem.at[2 * m + half]))
    for copy in copies:
        copy.start()
    for copy in copies:
        copy.wait()


def local(tokens, grad_output, gate_weight, up_weight, down_weight):
    anywhere = pl.BlockSpec(memory_space=pl.ANY)
    dma = pltpu.SemaphoreType.DMA
    sizes = [width for _, width in PHASES]
    vmem = pl.BlockSpec(memory_space=pltpu.VMEM)
    results = pl.pallas_call(
        kernel,
        out_shape=(
            pltpu.VMEM((32, 512), BF16),
            pltpu.VMEM((2, 2, 512, HALF), BF16),
            pltpu.VMEM((2, HALF, 512), BF16),
        ),
        in_specs=[anywhere] * 5,
        out_specs=(vmem, vmem, vmem),
        scratch_shapes=[
            pltpu.VMEM((2, 4, 4, 32, 512), BF16),
            pltpu.VMEM((2, 4, 4, 32, 512), BF16),
            pltpu.VMEM((2, 2, 512, HALF), BF16),
            pltpu.VMEM((2, HALF, 512), BF16),
            pltpu.VMEM((2, 512, HALF), BF16),
            pltpu.VMEM((HALF, 512), BF16),
            *[pltpu.VMEM((2, 3, 3, BLOCK, width), BF16) for width in sizes],
            *[pltpu.VMEM((2, 4, 3, BLOCK, width), BF16) for width in sizes],
            *[pltpu.VMEM((3, BLOCK, width), BF16) for width in sizes],
            *[pltpu.VMEM((3, BLOCK, width), F32) for width in sizes],
            *[pltpu.VMEM((2, 3, 512, width), BF16) for width in sizes],
            pltpu.VMEM((8, BLOCK, 512), BF16),
            pltpu.VMEM((16, 32, 512), BF16),
            dma((8,)),
            dma((3,)),
            dma((3,)),
            dma((2, 2, 9)),
            dma((2, 2, 9)),
            dma((2, 2, 4)),
            dma((2, 2, 4)),
            dma((2, 2, 4, 3)),
            dma((2, 2, 4, 3)),
            dma((2, 2, 4, 3)),
            dma((2, 2, 4, 3)),
            dma((2, 8)),
            dma((2, 8)),
            dma((8, 2)),
            dma((16,)),
        ],
        compiler_params=pltpu.CompilerParams(
            collective_id=0, has_side_effects=True, vmem_limit_bytes=55 * 2**20
        ),
        cost_estimate=pl.CostEstimate(flops=7_516_192_768, bytes_accessed=11_010_048, transcendentals=2_000_000),
    )(tokens, grad_output, gate_weight, up_weight, down_weight)
    return pl.pallas_call(
        write_out,
        out_shape=(
            jax.ShapeDtypeStruct((32, 512), BF16),
            jax.ShapeDtypeStruct((512, 1792), BF16),
            jax.ShapeDtypeStruct((512, 1792), BF16),
            jax.ShapeDtypeStruct((1792, 512), BF16),
        ),
        in_specs=[anywhere] * 3,
        out_specs=(anywhere,) * 4,
        scratch_shapes=[dma((7,))],
        compiler_params=pltpu.CompilerParams(vmem_limit_bytes=2**20),
    )(*results)


def solution(mesh):
    return jax.shard_map(
        local,
        mesh=mesh,
        in_specs=(
            P("hidden", "mp"),
            P("hidden", "mp"),
            P("mp", "hidden"),
            P("mp", "hidden"),
            P("hidden", "mp"),
        ),
        out_specs=(P("hidden", "mp"), P("mp", "hidden"), P("mp", "hidden"), P("hidden", "mp")),
        check_vma=False,
    )
```

```python
import jax
import jax.numpy as jnp
from jax import lax
from jax.experimental import pallas as pl
from jax.experimental.pallas import tpu as pltpu
from jax.sharding import PartitionSpec as P

MESH = pl.DeviceIdType.MESH
F32 = jnp.float32
BF16 = jnp.bfloat16
HALF = 896
SHARE = 16
ROW = 128
STEPS = (0, 1, 3, 2)
START = (0.0, 2.2, 2.3, 2.4)
SPREAD = (6.0, 6.55, 6.6, 6.75)


def encode(value):
    return (value * jnp.abs(value)).astype(BF16)


def decode(sent):
    square = sent.astype(F32)
    size = jnp.abs(square)
    root = size * lax.rsqrt(jnp.maximum(size, 1e-36))
    return jnp.where(square < 0, -root, root)


def dot_nt(left, right):
    return lax.dot_general(left, right, (((1,), (1,)), ((), ())), preferred_element_type=F32)


def dot_tn(left, right):
    return lax.dot_general(left, right, (((0,), (0,)), ((), ())), preferred_element_type=F32)


def kernel(
    tok_ref, go_ref, wg_ref, wu_ref, wd_ref,
    gi_ref, out_gu, out_d,
    act_in, act_px, w_gu, w_d, px_gu, px_d,
    part, rs_send, rs_recv, gathered, gi_send, gi_recv,
    load_sem, px_send, px_recv, tok_send, tok_recv, share_send, share_recv,
    rs_ssem, rs_rsem, ag_ssem, ag_rsem, pair_send, pair_recv, gi_ssem, gi_rsem,
):
    mp, hid = lax.axis_index("mp"), lax.axis_index("hidden")
    z, core = mp // 2, mp % 2
    y, x = hid // 4, hid % 4

    def remote(src, dst, ssem, rsem, device):
        return pltpu.make_async_remote_copy(
            src_ref=src, dst_ref=dst, send_sem=ssem, recv_sem=rsem, device_id=device, device_id_type=MESH
        )

    def ring(way):
        return (lax.rem(z + 1 + 6 * way, 8) * 2 + core, hid)

    partner = (z * 2 + (1 - core), hid)

    def in_plane(j):
        return (mp, lax.rem(hid + j, 16))

    def along_x(step):
        return (mp, y * 4 + lax.rem(x + step, 4))

    def along_y(step):
        return (mp, lax.rem(y + step, 4) * 4 + x)

    own_col = pl.multiple_of(core * HALF, 128)
    other_col = pl.multiple_of((1 - core) * HALF, 128)

    loads = []

    def load(src, dst):
        copy = pltpu.make_async_copy(src, dst, load_sem.at[len(loads)])
        copy.start()
        loads.append(copy)

    load(tok_ref, act_in.at[0, 0, x])
    load(go_ref, act_in.at[1, 0, x])
    for half, col in ((0, own_col), (1, other_col)):
        load(wg_ref.at[:, pl.ds(col, HALF)], w_gu.at[half, 0])
        load(wu_ref.at[:, pl.ds(col, HALF)], w_gu.at[half, 1])
        load(wd_ref.at[pl.ds(col, HALF), :], w_d.at[half])

    barrier = pltpu.get_barrier_semaphore()
    for j in range(1, 16):
        pl.semaphore_signal(barrier, inc=1, device_id=in_plane(j), device_id_type=MESH)
    for device in (ring(0), ring(1), partner):
        pl.semaphore_signal(barrier, inc=1, device_id=device, device_id_type=MESH)
    pl.semaphore_wait(barrier, 18)

    copies = []

    def begin(copy):
        copy.start()
        copies.append(copy)
        return copy

    low, high = slice(0, 256), slice(256, 512)
    row, column, wide, far, shares = {}, {}, {}, {}, {}
    for a, source in enumerate((tok_ref, go_ref)):
        for j, step in enumerate((2, 1, 3)):
            row[a, j] = begin(remote(
                source, act_in.at[a, 0, x], tok_send.at[a, j], tok_recv.at[a, j], along_x(step)
            ))
        for j, (step, q) in enumerate(((2, 3), (1, 2), (3, 1))):
            column[a, j] = begin(remote(
                source.at[:, high], act_in.at[a, q, x, :, high],
                tok_send.at[a, 3 + j], tok_recv.at[a, 3 + j], along_y(step),
            ))
    px_copies = []
    for i, (src, dst) in enumerate((
        (wg_ref.at[:, pl.ds(other_col, HALF)], px_gu.at[0]),
        (wu_ref.at[:, pl.ds(other_col, HALF)], px_gu.at[1]),
        (wd_ref.at[pl.ds(other_col, HALF), :], px_d),
    )):
        px_copies.append(begin(remote(src, dst, px_send.at[i], px_recv.at[i], partner)))

    def share(a, i):
        q = slice(0, 1) if i == 0 else slice(1, 4)
        shares[a, i] = begin(remote(
            act_in.at[a, q], act_px.at[a, q], share_send.at[a, i], share_recv.at[a, i], partner
        ))

    def send_row(a):
        loads[a].wait()
        for j in range(3):
            row[a, j].wait_recv()
        share(a, 0)
        for way in (a, 1 - a):
            wide[a, 0, way] = begin(remote(
                act_in.at[a, 0, :, :, low], act_in.at[a, 2 - way, :, :, low],
                tok_send.at[a, 6 + way], tok_recv.at[a, 6 + way], along_y(1 + 2 * way),
            ))

    def send_column(a):
        for j in range(3):
            column[a, j].wait_recv()
        for way in (a, 1 - a):
            ref = act_in.at[a, 1:4, x, :, high]
            wide[a, 1, way] = begin(remote(
                ref, ref, tok_send.at[a, 8 + way], tok_recv.at[a, 8 + way], along_x(1 + 2 * way)
            ))

    def pass_on(a):
        wide[a, 0, a].wait_recv()
        far[a, 0] = begin(remote(
            act_in.at[a, 2 - a, :, :, low], act_in.at[a, 3, :, :, low],
            tok_send.at[a, 10], tok_recv.at[a, 10], along_y(1 + 2 * a),
        ))
        wide[a, 1, a].wait_recv()
        ref = act_in.at[a, 1:4, lax.rem(x + 3 - 2 * a, 4), :, high]
        far[a, 1] = begin(remote(ref, ref, tok_send.at[a, 11], tok_recv.at[a, 11], along_x(1 + 2 * a)))

    def share_far(a):
        for axis in range(2):
            wide[a, axis, 1 - a].wait_recv()
            far[a, axis].wait_recv()
        share(a, 1)

    def multiply(q):
        for m in range(3):
            a = m // 2
            if m != 1 and q < 2:
                shares[a, q].wait_recv()
            ours, theirs = act_in[a, q].reshape(ROW, 512), act_px[a, q].reshape(ROW, 512)
            if q == 0:
                px_copies[m].wait_recv()
            if m == 2:
                part[q, m] = dot_nt(ours, w_d[0]) + dot_nt(theirs, px_d[...])
            else:
                part[q, m] = jnp.dot(ours, w_gu[0, m], preferred_element_type=F32) + jnp.dot(
                    theirs, px_gu[m], preferred_element_type=F32
                )

    def sum_copy(q, way, step):
        return remote(
            rs_send.at[q, way, step], rs_recv.at[q, way, step],
            rs_ssem.at[q, way, step], rs_rsem.at[q, way, step], ring(way),
        )

    def sum_ways(q, step):
        return (q % 2,) if step == 0 else (q % 2, 1 - q % 2)

    def reduce(q, step):
        for way in sum_ways(q, step):
            distance = 4 - step
            d = lax.rem(z + (distance if way == 0 else 8 - distance), 8)
            total = part[q, :, pl.ds(pl.multiple_of(d * SHARE, SHARE), SHARE)]
            if step > 0 and way in sum_ways(q, step - 1):
                sum_copy(q, way, step - 1).wait_recv()
                total += decode(rs_recv[q, way, step - 1])
            rs_send[q, way, step] = encode(total)
            sum_copy(q, way, step).start()

    def rows(q, d):
        return pl.ds(pl.multiple_of(q * ROW + d * SHARE, SHARE), SHARE)

    def activate(q):
        sums = part[q, :, pl.ds(pl.multiple_of(z * SHARE, SHARE), SHARE)]
        for way in sum_ways(q, 3):
            sum_copy(q, way, 3).wait_recv()
            sums += decode(rs_recv[q, way, 3])
        gate, up, grad_hidden = sums[0], sums[1], sums[2]
        sig = jax.nn.sigmoid(gate)
        silu_gate = gate * sig
        gathered[0, 0, rows(q, z)] = (silu_gate * up).astype(BF16)
        gathered[0, 1, rows(q, z)] = (grad_hidden * up * sig * (1.0 + gate * (1.0 - sig))).astype(BF16)
        gathered[0, 2, rows(q, z)] = (grad_hidden * silu_gate).astype(BF16)

    def spread_copy(q, way, step):
        ref = gathered.at[0, :, rows(q, lax.rem(z + (8 - step if way == 0 else step), 8))]
        return remote(ref, ref, ag_ssem.at[q, way, step], ag_rsem.at[q, way, step], ring(way))

    def spread_ways(q, step):
        return (q % 2,) if step == 3 else (q % 2, 1 - q % 2)

    def pair_copy(q, k):
        at = rows(q, lax.rem(z + (0, 7, 6, 5, 1, 2, 3, 4)[k], 8))
        return remote(
            gathered.at[0, :, at], gathered.at[1, :, at], pair_send.at[q, k], pair_recv.at[q, k], partner
        )

    def spread(q, step):
        if step == 0:
            activate(q)
        for way in (q % 2, 1 - q % 2):
            if 0 < step < 4 or (step == 4 and way == q % 2):
                spread_copy(q, way, step - 1).wait_recv()
            if step < 4 and way in spread_ways(q, step):
                spread_copy(q, way, step).start()
        if step == 0:
            pair_copy(q, 0).start()
        elif step < 4:
            pair_copy(q, step).start()
            pair_copy(q, 3 + step).start()
        else:
            pair_copy(q, 7).start()

    def gi_copy(q, d):
        return remote(
            gi_send.at[d, q], gi_recv.at[hid, lax.rem(d, 2)], gi_ssem.at[d, q],
            gi_rsem.at[hid, lax.rem(d, 2)], (mp, lax.rem(y + STEPS[q], 4) * 4 + d // 2),
        )

    def gi_each(q, d, act):
        if q == 0:
            pl.when(x != d // 2)(lambda: act(gi_copy(q, d)))
        else:
            act(gi_copy(q, d))

    def input_grad(distance):
        places = ((0, z),) if distance == 0 else ((7, lax.rem(z + 4, 8)),) if distance == 4 else (
            (distance, lax.rem(z + 8 - distance, 8)), (3 + distance, lax.rem(z + distance, 8))
        )
        for k, _ in places:
            for q in range(4):
                pair_copy(q, k).wait_recv()
        total = jnp.zeros((4 * SHARE * len(places), 512), F32)
        for half in range(2):
            for mat in range(2):
                left = jnp.concatenate([gathered[half, 1 + mat, rows(q, d)] for _, d in places for q in range(4)])
                total += dot_nt(left, w_gu[half, mat])
        for i, (_, d) in enumerate(places):
            for q in range(4):
                start = (4 * i + q) * SHARE
                gi_send[d, q] = encode(total[start : start + SHARE])
                gi_each(q, d, lambda copy: copy.start())

    def saliency(half, _):
        tokens = act_in[0].reshape(512, 512)
        for mat in range(2):
            for cols in (slice(0, 512), slice(512, HALF)):
                grads = dot_tn(tokens, gathered[half, 1 + mat, :, cols])
                out_gu[half, mat, :, cols] = jnp.abs(w_gu[half, mat, :, cols].astype(F32) * grads).astype(BF16)
        for cols in (slice(0, 512), slice(512, HALF)):
            grads = dot_tn(gathered[half, 0, :, cols], act_in[1].reshape(512, 512))
            out_d[half, cols, :] = jnp.abs(w_d[half, cols, :].astype(F32) * grads).astype(BF16)
        return 0

    send_row(0)
    send_row(1)
    for copy in loads[2:]:
        copy.wait()
    events = [
        (-0.05, 0, lambda: (send_column(0), send_column(1))),
        (0.9, 0, lambda: (pass_on(0), pass_on(1))),
        (1.9, 0, lambda: (share_far(0), share_far(1))),
    ]
    for q in range(4):
        events.append((START[q] - 0.1, q, lambda q=q: multiply(q)))
        for step in range(4):
            events.append((START[q] + step, q, lambda q=q, step=step: reduce(q, step)))
        for step in range(5):
            events.append((SPREAD[q] + step, q, lambda q=q, step=step: spread(q, step)))
    for distance, when in enumerate((1.05, 2.05, 3.05, 3.5, 4.5)):
        events.append((SPREAD[3] + when, 4, lambda distance=distance: input_grad(distance)))
    for _, _, event in sorted(events, key=lambda e: e[:2]):
        event()
    lax.fori_loop(0, 2, saliency, 0)

    totals = [decode(gi_send[2 * x + i, 0]) for i in range(2)]
    for j in range(1, 16):
        slot = lax.rem(hid + j, 16)
        for i in range(2):
            remote(
                gi_send.at[0, 0], gi_recv.at[slot, i], gi_ssem.at[0, 0], gi_rsem.at[slot, i], in_plane(j)
            ).wait_recv()
            totals[i] += decode(gi_recv[slot, i])
    for i in range(2):
        gi_ref[SHARE * i : SHARE * i + SHARE] = totals[i].astype(BF16)

    for copy in copies:
        copy.wait_send()
    for q in range(4):
        for step in range(4):
            for way in sum_ways(q, step):
                sum_copy(q, way, step).wait_send()
            for way in spread_ways(q, step):
                spread_copy(q, way, step).wait_send()
        for k in range(8):
            pair_copy(q, k).wait_send()
        for d in range(8):
            gi_each(q, d, lambda copy: copy.wait_send())


def write_out(gi_in, gu_in, d_in, gi_ref, sg_ref, su_ref, sd_ref, sem):
    core = lax.rem(lax.axis_index("mp"), 2)
    copies = [pltpu.make_async_copy(gi_in, gi_ref, sem.at[6])]
    for half in range(2):
        at = pl.ds(pl.multiple_of((core + half * (1 - 2 * core)) * HALF, 128), HALF)
        for m, (src, dst) in enumerate((
            (gu_in.at[half, 0], sg_ref.at[:, at]),
            (gu_in.at[half, 1], su_ref.at[:, at]),
            (d_in.at[half], sd_ref.at[at, :]),
        )):
            copies.append(pltpu.make_async_copy(src, dst, sem.at[2 * m + half]))
    for copy in copies:
        copy.start()
    for copy in copies:
        copy.wait()


def local(tokens, grad_output, gate_weight, up_weight, down_weight):
    anywhere = pl.BlockSpec(memory_space=pl.ANY)
    dma = pltpu.SemaphoreType.DMA
    vmem = pl.BlockSpec(memory_space=pltpu.VMEM)
    results = pl.pallas_call(
        kernel,
        out_shape=(
            pltpu.VMEM((32, 512), BF16),
            pltpu.VMEM((2, 2, 512, HALF), BF16),
            pltpu.VMEM((2, HALF, 512), BF16),
        ),
        in_specs=[anywhere] * 5,
        out_specs=(vmem, vmem, vmem),
        scratch_shapes=[
            pltpu.VMEM((2, 4, 4, 32, 512), BF16),
            pltpu.VMEM((2, 4, 4, 32, 512), BF16),
            pltpu.VMEM((2, 2, 512, HALF), BF16),
            pltpu.VMEM((2, HALF, 512), BF16),
            pltpu.VMEM((2, 512, HALF), BF16),
            pltpu.VMEM((HALF, 512), BF16),
            pltpu.VMEM((4, 3, ROW, HALF), F32),
            pltpu.VMEM((4, 2, 4, 3, SHARE, HALF), BF16),
            pltpu.VMEM((4, 2, 4, 3, SHARE, HALF), BF16),
            pltpu.VMEM((2, 3, 512, HALF), BF16),
            pltpu.VMEM((8, 4, SHARE, 512), BF16),
            pltpu.VMEM((16, 2, SHARE, 512), BF16),
            dma((8,)),
            dma((3,)),
            dma((3,)),
            dma((2, 12)),
            dma((2, 12)),
            dma((2, 2)),
            dma((2, 2)),
            dma((4, 2, 4)),
            dma((4, 2, 4)),
            dma((4, 2, 4)),
            dma((4, 2, 4)),
            dma((4, 8)),
            dma((4, 8)),
            dma((8, 4)),
            dma((16, 2)),
        ],
        compiler_params=pltpu.CompilerParams(
            collective_id=0, has_side_effects=True, vmem_limit_bytes=55 * 2**20
        ),
        cost_estimate=pl.CostEstimate(flops=7_516_192_768, bytes_accessed=11_010_048, transcendentals=2_000_000),
    )(tokens, grad_output, gate_weight, up_weight, down_weight)
    return pl.pallas_call(
        write_out,
        out_shape=(
            jax.ShapeDtypeStruct((32, 512), BF16),
            jax.ShapeDtypeStruct((512, 1792), BF16),
            jax.ShapeDtypeStruct((512, 1792), BF16),
            jax.ShapeDtypeStruct((1792, 512), BF16),
        ),
        in_specs=[anywhere] * 3,
        out_specs=(anywhere,) * 4,
        scratch_shapes=[dma((7,))],
        compiler_params=pltpu.CompilerParams(vmem_limit_bytes=2**20),
    )(*results)


def solution(mesh):
    return jax.shard_map(
        local,
        mesh=mesh,
        in_specs=(
            P("hidden", "mp"),
            P("hidden", "mp"),
            P("mp", "hidden"),
            P("mp", "hidden"),
            P("hidden", "mp"),
        ),
        out_specs=(P("hidden", "mp"), P("mp", "hidden"), P("mp", "hidden"), P("hidden", "mp")),
        check_vma=False,
    )
```

```python
import jax
import jax.numpy as jnp
from jax import lax
from jax.experimental import pallas as pl
from jax.experimental.pallas import tpu as pltpu
from jax.sharding import PartitionSpec as P

MESH = pl.DeviceIdType.MESH
F32 = jnp.float32
BF16 = jnp.bfloat16
HALF = 896
SHARE = 16
ROW = 128
STEPS = (0, 1, 3, 2)
START = (0.0, 2.2, 2.3, 2.4)
SPREAD = (6.0, 6.55, 6.6, 6.75)


def encode(value):
    return (value * jnp.abs(value)).astype(BF16)


def decode(sent):
    square = sent.astype(F32)
    size = jnp.abs(square)
    root = size * lax.rsqrt(jnp.maximum(size, 1e-36))
    return jnp.where(square < 0, -root, root)


def dot_nt(left, right):
    return lax.dot_general(left, right, (((1,), (1,)), ((), ())), preferred_element_type=F32)


def dot_tn(left, right):
    return lax.dot_general(left, right, (((0,), (0,)), ((), ())), preferred_element_type=F32)


def kernel(
    tok_ref, go_ref, wg_ref, wu_ref, wd_ref,
    gi_ref, out_gu, out_d,
    act_in, act_px, w_gu, w_d, px_gu, px_d,
    part, rs_send, rs_recv, gathered, gi_send, gi_recv,
    load_sem, px_send, px_recv, tok_send, tok_recv, share_send, share_recv,
    rs_ssem, rs_rsem, ag_ssem, ag_rsem, pair_send, pair_recv, gi_ssem, gi_rsem,
):
    mp, hid = lax.axis_index("mp"), lax.axis_index("hidden")
    z, core = mp // 2, mp % 2
    y, x = hid // 4, hid % 4

    def remote(src, dst, ssem, rsem, device):
        return pltpu.make_async_remote_copy(
            src_ref=src, dst_ref=dst, send_sem=ssem, recv_sem=rsem, device_id=device, device_id_type=MESH
        )

    def ring(way):
        return (lax.rem(z + 1 + 6 * way, 8) * 2 + core, hid)

    partner = (z * 2 + (1 - core), hid)

    def in_plane(j):
        return (mp, lax.rem(hid + j, 16))

    def along_x(step):
        return (mp, y * 4 + lax.rem(x + step, 4))

    def along_y(step):
        return (mp, lax.rem(y + step, 4) * 4 + x)

    own_col = pl.multiple_of(core * HALF, 128)
    other_col = pl.multiple_of((1 - core) * HALF, 128)

    loads = []

    def load(src, dst):
        copy = pltpu.make_async_copy(src, dst, load_sem.at[len(loads)])
        copy.start()
        loads.append(copy)

    load(tok_ref, act_in.at[0, 0, x])
    load(go_ref, act_in.at[1, 0, x])
    def load_half(half, col):
        load(wg_ref.at[:, pl.ds(col, HALF)], w_gu.at[half, 0])
        load(wu_ref.at[:, pl.ds(col, HALF)], w_gu.at[half, 1])
        load(wd_ref.at[pl.ds(col, HALF), :], w_d.at[half])

    load_half(0, own_col)

    barrier = pltpu.get_barrier_semaphore()
    for j in range(1, 16):
        pl.semaphore_signal(barrier, inc=1, device_id=in_plane(j), device_id_type=MESH)
    for device in (ring(0), ring(1), partner):
        pl.semaphore_signal(barrier, inc=1, device_id=device, device_id_type=MESH)
    pl.semaphore_wait(barrier, 18)

    copies = []

    def begin(copy):
        copy.start()
        copies.append(copy)
        return copy

    low, high = slice(0, 256), slice(256, 512)
    row, column, wide, far, shares = {}, {}, {}, {}, {}
    for a, source in enumerate((tok_ref, go_ref)):
        for j, step in enumerate((2, 1, 3)):
            row[a, j] = begin(remote(
                source, act_in.at[a, 0, x], tok_send.at[a, j], tok_recv.at[a, j], along_x(step)
            ))
    for a, source in enumerate((tok_ref, go_ref)):
        for j, (step, q) in enumerate(((2, 3), (1, 2), (3, 1))):
            column[a, j] = begin(remote(
                source.at[:, high], act_in.at[a, q, x, :, high],
                tok_send.at[a, 3 + j], tok_recv.at[a, 3 + j], along_y(step),
            ))
    px_copies = []
    for i, (src, dst) in enumerate((
        (wg_ref.at[:, pl.ds(other_col, HALF)], px_gu.at[0]),
        (wu_ref.at[:, pl.ds(other_col, HALF)], px_gu.at[1]),
        (wd_ref.at[pl.ds(other_col, HALF), :], px_d),
    )):
        px_copies.append(begin(remote(src, dst, px_send.at[i], px_recv.at[i], partner)))

    def share(a, i):
        q = slice(0, 1) if i == 0 else slice(1, 4)
        shares[a, i] = begin(remote(
            act_in.at[a, q], act_px.at[a, q], share_send.at[a, i], share_recv.at[a, i], partner
        ))

    def send_row(a):
        loads[a].wait()
        for j in range(3):
            row[a, j].wait_recv()
        share(a, 0)
        for way in (a, 1 - a):
            wide[a, 0, way] = begin(remote(
                act_in.at[a, 0, :, :, low], act_in.at[a, 2 - way, :, :, low],
                tok_send.at[a, 6 + way], tok_recv.at[a, 6 + way], along_y(1 + 2 * way),
            ))

    def send_column(a):
        for j in range(3):
            column[a, j].wait_recv()
        for way in (a, 1 - a):
            ref = act_in.at[a, 1:4, x, :, high]
            wide[a, 1, way] = begin(remote(
                ref, ref, tok_send.at[a, 8 + way], tok_recv.at[a, 8 + way], along_x(1 + 2 * way)
            ))

    def pass_on(a):
        wide[a, 0, a].wait_recv()
        far[a, 0] = begin(remote(
            act_in.at[a, 2 - a, :, :, low], act_in.at[a, 3, :, :, low],
            tok_send.at[a, 10], tok_recv.at[a, 10], along_y(1 + 2 * a),
        ))
        wide[a, 1, a].wait_recv()
        ref = act_in.at[a, 1:4, lax.rem(x + 3 - 2 * a, 4), :, high]
        far[a, 1] = begin(remote(ref, ref, tok_send.at[a, 11], tok_recv.at[a, 11], along_x(1 + 2 * a)))

    def share_far(a):
        for axis in range(2):
            wide[a, axis, 1 - a].wait_recv()
            far[a, axis].wait_recv()
        share(a, 1)

    def multiply(q):
        for m in range(3):
            a = m // 2
            if m != 1 and q < 2:
                shares[a, q].wait_recv()
            ours, theirs = act_in[a, q].reshape(ROW, 512), act_px[a, q].reshape(ROW, 512)
            if q == 0:
                px_copies[m].wait_recv()
            if m == 2:
                part[q, m] = dot_nt(ours, w_d[0]) + dot_nt(theirs, px_d[...])
            else:
                part[q, m] = jnp.dot(ours, w_gu[0, m], preferred_element_type=F32) + jnp.dot(
                    theirs, px_gu[m], preferred_element_type=F32
                )

    def sum_copy(q, way, step):
        return remote(
            rs_send.at[q, way, step], rs_recv.at[q, way, step],
            rs_ssem.at[q, way, step], rs_rsem.at[q, way, step], ring(way),
        )

    def sum_ways(q, step):
        return (q % 2,) if step == 0 else (q % 2, 1 - q % 2)

    def reduce(q, step):
        for way in sum_ways(q, step):
            distance = 4 - step
            d = lax.rem(z + (distance if way == 0 else 8 - distance), 8)
            total = part[q, :, pl.ds(pl.multiple_of(d * SHARE, SHARE), SHARE)]
            if step > 0 and way in sum_ways(q, step - 1):
                sum_copy(q, way, step - 1).wait_recv()
                total += decode(rs_recv[q, way, step - 1])
            rs_send[q, way, step] = encode(total)
            sum_copy(q, way, step).start()

    def rows(q, d):
        return pl.ds(pl.multiple_of(q * ROW + d * SHARE, SHARE), SHARE)

    def activate(q):
        sums = part[q, :, pl.ds(pl.multiple_of(z * SHARE, SHARE), SHARE)]
        for way in sum_ways(q, 3):
            sum_copy(q, way, 3).wait_recv()
            sums += decode(rs_recv[q, way, 3])
        gate, up, grad_hidden = sums[0], sums[1], sums[2]
        sig = jax.nn.sigmoid(gate)
        silu_gate = gate * sig
        gathered[0, 0, rows(q, z)] = (silu_gate * up).astype(BF16)
        gathered[0, 1, rows(q, z)] = (grad_hidden * up * sig * (1.0 + gate * (1.0 - sig))).astype(BF16)
        gathered[0, 2, rows(q, z)] = (grad_hidden * silu_gate).astype(BF16)

    def spread_copy(q, way, step):
        ref = gathered.at[0, :, rows(q, lax.rem(z + (8 - step if way == 0 else step), 8))]
        return remote(ref, ref, ag_ssem.at[q, way, step], ag_rsem.at[q, way, step], ring(way))

    def spread_ways(q, step):
        return (q % 2,) if step == 3 else (q % 2, 1 - q % 2)

    def pair_copy(q, k):
        at = rows(q, lax.rem(z + (0, 7, 6, 5, 1, 2, 3, 4)[k], 8))
        return remote(
            gathered.at[0, :, at], gathered.at[1, :, at], pair_send.at[q, k], pair_recv.at[q, k], partner
        )

    def spread(q, step):
        if step == 0:
            activate(q)
        for way in (q % 2, 1 - q % 2):
            if 0 < step < 4 or (step == 4 and way == q % 2):
                spread_copy(q, way, step - 1).wait_recv()
            if step < 4 and way in spread_ways(q, step):
                spread_copy(q, way, step).start()
        if step == 0:
            pair_copy(q, 0).start()
        elif step < 4:
            pair_copy(q, step).start()
            pair_copy(q, 3 + step).start()
        else:
            pair_copy(q, 7).start()

    def gi_copy(q, d):
        return remote(
            gi_send.at[d, q], gi_recv.at[hid, lax.rem(d, 2)], gi_ssem.at[d, q],
            gi_rsem.at[hid, lax.rem(d, 2)], (mp, lax.rem(y + STEPS[q], 4) * 4 + d // 2),
        )

    def gi_each(q, d, act):
        if q == 0:
            pl.when(x != d // 2)(lambda: act(gi_copy(q, d)))
        else:
            act(gi_copy(q, d))

    def input_grad(distance):
        places = ((0, z),) if distance == 0 else ((7, lax.rem(z + 4, 8)),) if distance == 4 else (
            (distance, lax.rem(z + 8 - distance, 8)), (3 + distance, lax.rem(z + distance, 8))
        )
        for k, _ in places:
            for q in range(4):
                pair_copy(q, k).wait_recv()
        total = jnp.zeros((4 * SHARE * len(places), 512), F32)
        for half in range(2):
            for mat in range(2):
                left = jnp.concatenate([gathered[half, 1 + mat, rows(q, d)] for _, d in places for q in range(4)])
                total += dot_nt(left, w_gu[half, mat])
        for i, (_, d) in enumerate(places):
            for q in range(4):
                start = (4 * i + q) * SHARE
                gi_send[d, q] = encode(total[start : start + SHARE])
                gi_each(q, d, lambda copy: copy.start())

    def saliency_in(half, mat):
        tokens = act_in[0].reshape(512, 512)
        for cols in (slice(0, 512), slice(512, HALF)):
            grads = dot_tn(tokens, gathered[half, 1 + mat, :, cols])
            out_gu[half, mat, :, cols] = jnp.abs(w_gu[half, mat, :, cols].astype(F32) * grads).astype(BF16)

    def saliency_down(half):
        for cols in (slice(0, 512), slice(512, HALF)):
            grads = dot_tn(gathered[half, 0, :, cols], act_in[1].reshape(512, 512))
            out_d[half, cols, :] = jnp.abs(w_d[half, cols, :].astype(F32) * grads).astype(BF16)

    send_row(0)
    send_row(1)
    for copy in loads[2:]:
        copy.wait()
    load_half(1, other_col)
    events = [
        (4.0, 0, lambda: [copy.wait() for copy in loads[5:]]),
        (-0.05, 0, lambda: (send_column(0), send_column(1))),
        (0.9, 0, lambda: (pass_on(0), pass_on(1))),
        (1.9, 0, lambda: (share_far(0), share_far(1))),
    ]
    for q in range(4):
        events.append((START[q] - 0.1, q, lambda q=q: multiply(q)))
        for step in range(4):
            events.append((START[q] + step, q, lambda q=q, step=step: reduce(q, step)))
        for step in range(5):
            events.append((SPREAD[q] + step, q, lambda q=q, step=step: spread(q, step)))
    for distance, when in enumerate((1.05, 2.05, 3.05, 3.5, 4.5)):
        events.append((SPREAD[3] + when, 4, lambda distance=distance: input_grad(distance)))
    events.append((SPREAD[3] + 4.2, 4, lambda: (saliency_in(0, 0), saliency_in(0, 1))))
    for _, _, event in sorted(events, key=lambda e: e[:2]):
        event()
    saliency_down(0)
    for mat in range(2):
        saliency_in(1, mat)
    saliency_down(1)

    totals = [decode(gi_send[2 * x + i, 0]) for i in range(2)]
    for j in range(1, 16):
        slot = lax.rem(hid + j, 16)
        for i in range(2):
            remote(
                gi_send.at[0, 0], gi_recv.at[slot, i], gi_ssem.at[0, 0], gi_rsem.at[slot, i], in_plane(j)
            ).wait_recv()
            totals[i] += decode(gi_recv[slot, i])
    for i in range(2):
        gi_ref[SHARE * i : SHARE * i + SHARE] = totals[i].astype(BF16)

    for copy in copies:
        copy.wait_send()
    for q in range(4):
        for step in range(4):
            for way in sum_ways(q, step):
                sum_copy(q, way, step).wait_send()
            for way in spread_ways(q, step):
                spread_copy(q, way, step).wait_send()
        for k in range(8):
            pair_copy(q, k).wait_send()
        for d in range(8):
            gi_each(q, d, lambda copy: copy.wait_send())


def write_out(gi_in, gu_in, d_in, gi_ref, sg_ref, su_ref, sd_ref, sem):
    core = lax.rem(lax.axis_index("mp"), 2)
    copies = [pltpu.make_async_copy(gi_in, gi_ref, sem.at[6])]
    for half in range(2):
        at = pl.ds(pl.multiple_of((core + half * (1 - 2 * core)) * HALF, 128), HALF)
        for m, (src, dst) in enumerate((
            (gu_in.at[half, 0], sg_ref.at[:, at]),
            (gu_in.at[half, 1], su_ref.at[:, at]),
            (d_in.at[half], sd_ref.at[at, :]),
        )):
            copies.append(pltpu.make_async_copy(src, dst, sem.at[2 * m + half]))
    for copy in copies:
        copy.start()
    for copy in copies:
        copy.wait()


def local(tokens, grad_output, gate_weight, up_weight, down_weight):
    anywhere = pl.BlockSpec(memory_space=pl.ANY)
    dma = pltpu.SemaphoreType.DMA
    vmem = pl.BlockSpec(memory_space=pltpu.VMEM)
    results = pl.pallas_call(
        kernel,
        out_shape=(
            pltpu.VMEM((32, 512), BF16),
            pltpu.VMEM((2, 2, 512, HALF), BF16),
            pltpu.VMEM((2, HALF, 512), BF16),
        ),
        in_specs=[anywhere] * 5,
        out_specs=(vmem, vmem, vmem),
        scratch_shapes=[
            pltpu.VMEM((2, 4, 4, 32, 512), BF16),
            pltpu.VMEM((2, 4, 4, 32, 512), BF16),
            pltpu.VMEM((2, 2, 512, HALF), BF16),
            pltpu.VMEM((2, HALF, 512), BF16),
            pltpu.VMEM((2, 512, HALF), BF16),
            pltpu.VMEM((HALF, 512), BF16),
            pltpu.VMEM((4, 3, ROW, HALF), F32),
            pltpu.VMEM((4, 2, 4, 3, SHARE, HALF), BF16),
            pltpu.VMEM((4, 2, 4, 3, SHARE, HALF), BF16),
            pltpu.VMEM((2, 3, 512, HALF), BF16),
            pltpu.VMEM((8, 4, SHARE, 512), BF16),
            pltpu.VMEM((16, 2, SHARE, 512), BF16),
            dma((8,)),
            dma((3,)),
            dma((3,)),
            dma((2, 12)),
            dma((2, 12)),
            dma((2, 2)),
            dma((2, 2)),
            dma((4, 2, 4)),
            dma((4, 2, 4)),
            dma((4, 2, 4)),
            dma((4, 2, 4)),
            dma((4, 8)),
            dma((4, 8)),
            dma((8, 4)),
            dma((16, 2)),
        ],
        compiler_params=pltpu.CompilerParams(
            collective_id=0, has_side_effects=True, vmem_limit_bytes=55 * 2**20
        ),
        cost_estimate=pl.CostEstimate(flops=7_516_192_768, bytes_accessed=11_010_048, transcendentals=2_000_000),
    )(tokens, grad_output, gate_weight, up_weight, down_weight)
    return pl.pallas_call(
        write_out,
        out_shape=(
            jax.ShapeDtypeStruct((32, 512), BF16),
            jax.ShapeDtypeStruct((512, 1792), BF16),
            jax.ShapeDtypeStruct((512, 1792), BF16),
            jax.ShapeDtypeStruct((1792, 512), BF16),
        ),
        in_specs=[anywhere] * 3,
        out_specs=(anywhere,) * 4,
        scratch_shapes=[dma((7,))],
        compiler_params=pltpu.CompilerParams(vmem_limit_bytes=2**20),
    )(*results)


def solution(mesh):
    return jax.shard_map(
        local,
        mesh=mesh,
        in_specs=(
            P("hidden", "mp"),
            P("hidden", "mp"),
            P("mp", "hidden"),
            P("mp", "hidden"),
            P("hidden", "mp"),
        ),
        out_specs=(P("hidden", "mp"), P("mp", "hidden"), P("mp", "hidden"), P("hidden", "mp")),
        check_vma=False,
    )
```

```python
import jax
import jax.numpy as jnp
from jax import lax
from jax.experimental import pallas as pl
from jax.experimental.pallas import tpu as pltpu
from jax.sharding import PartitionSpec as P

MESH = pl.DeviceIdType.MESH
F32 = jnp.float32
BF16 = jnp.bfloat16
HALF = 896
SHARE = 16
ROW = 128
STEPS = (0, 1, 3, 2)
START = (0.0, 2.2, 2.3, 2.4)
SPREAD = (6.0, 6.55, 6.6, 6.75)


def encode(value):
    return (value * jnp.abs(value)).astype(BF16)


def decode(sent):
    square = sent.astype(F32)
    size = jnp.abs(square)
    root = size * lax.rsqrt(jnp.maximum(size, 1e-36))
    return jnp.where(square < 0, -root, root)


def dot_nt(left, right):
    return lax.dot_general(left, right, (((1,), (1,)), ((), ())), preferred_element_type=F32)


def dot_tn(left, right):
    return lax.dot_general(left, right, (((0,), (0,)), ((), ())), preferred_element_type=F32)


def kernel(
    tok_ref, go_ref, wg_ref, wu_ref, wd_ref,
    gi_ref, out_gu, out_d,
    act_in, act_px, w_gu, w_d, px_gu, px_d,
    part, rs_send, rs_recv, gathered, gi_send, gi_recv,
    load_sem, px_send, px_recv, tok_send, tok_recv, share_send, share_recv,
    rs_ssem, rs_rsem, ag_ssem, ag_rsem, pair_send, pair_recv, gi_ssem, gi_rsem,
):
    mp, hid = lax.axis_index("mp"), lax.axis_index("hidden")
    z, core = mp // 2, mp % 2
    y, x = hid // 4, hid % 4

    def remote(src, dst, ssem, rsem, device):
        return pltpu.make_async_remote_copy(
            src_ref=src, dst_ref=dst, send_sem=ssem, recv_sem=rsem, device_id=device, device_id_type=MESH
        )

    def ring(way):
        return (lax.rem(z + 1 + 6 * way, 8) * 2 + core, hid)

    partner = (z * 2 + (1 - core), hid)

    def in_plane(j):
        return (mp, lax.rem(hid + j, 16))

    def along_x(step):
        return (mp, y * 4 + lax.rem(x + step, 4))

    def along_y(step):
        return (mp, lax.rem(y + step, 4) * 4 + x)

    own_col = pl.multiple_of(core * HALF, 128)
    other_col = pl.multiple_of((1 - core) * HALF, 128)

    loads = []

    def load(src, dst):
        copy = pltpu.make_async_copy(src, dst, load_sem.at[len(loads)])
        copy.start()
        loads.append(copy)

    load(tok_ref, act_in.at[0, 0, x])
    load(go_ref, act_in.at[1, 0, x])
    def load_half(half, col):
        load(wg_ref.at[:, pl.ds(col, HALF)], w_gu.at[half, 0])
        load(wu_ref.at[:, pl.ds(col, HALF)], w_gu.at[half, 1])
        load(wd_ref.at[pl.ds(col, HALF), :], w_d.at[half])

    load_half(0, own_col)

    barrier = pltpu.get_barrier_semaphore()
    for j in range(1, 16):
        pl.semaphore_signal(barrier, inc=1, device_id=in_plane(j), device_id_type=MESH)
    for device in (ring(0), ring(1), partner):
        pl.semaphore_signal(barrier, inc=1, device_id=device, device_id_type=MESH)
    pl.semaphore_wait(barrier, 18)

    copies = []

    def begin(copy):
        copy.start()
        copies.append(copy)
        return copy

    low, high = slice(0, 256), slice(256, 512)
    row, column, wide, far, shares = {}, {}, {}, {}, {}
    for a, source in enumerate((tok_ref, go_ref)):
        for j, step in enumerate((2, 1, 3)):
            row[a, j] = begin(remote(
                source, act_in.at[a, 0, x], tok_send.at[a, j], tok_recv.at[a, j], along_x(step)
            ))
    for a, source in enumerate((tok_ref, go_ref)):
        for j, (step, q) in enumerate(((2, 3), (1, 2), (3, 1))):
            column[a, j] = begin(remote(
                source.at[:, high], act_in.at[a, q, x, :, high],
                tok_send.at[a, 3 + j], tok_recv.at[a, 3 + j], along_y(step),
            ))
    px_copies = []

    def exchange(src, dst):
        i = len(px_copies)
        px_copies.append(begin(remote(src, dst, px_send.at[i], px_recv.at[i], partner)))

    exchange(wg_ref.at[:, pl.ds(other_col, HALF)], px_gu.at[0])
    exchange(wu_ref.at[:, pl.ds(other_col, HALF)], px_gu.at[1])

    def share(a, i):
        q = slice(0, 1) if i == 0 else slice(1, 4)
        shares[a, i] = begin(remote(
            act_in.at[a, q], act_px.at[a, q], share_send.at[a, i], share_recv.at[a, i], partner
        ))

    def send_row(a):
        loads[a].wait()
        for j in range(3):
            row[a, j].wait_recv()
        share(a, 0)
        for way in (a, 1 - a):
            wide[a, 0, way] = begin(remote(
                act_in.at[a, 0, :, :, low], act_in.at[a, 2 - way, :, :, low],
                tok_send.at[a, 6 + way], tok_recv.at[a, 6 + way], along_y(1 + 2 * way),
            ))

    def send_column(a):
        for j in range(3):
            column[a, j].wait_recv()
        for way in (a, 1 - a):
            ref = act_in.at[a, 1:4, x, :, high]
            wide[a, 1, way] = begin(remote(
                ref, ref, tok_send.at[a, 8 + way], tok_recv.at[a, 8 + way], along_x(1 + 2 * way)
            ))

    def pass_on(a):
        wide[a, 0, a].wait_recv()
        far[a, 0] = begin(remote(
            act_in.at[a, 2 - a, :, :, low], act_in.at[a, 3, :, :, low],
            tok_send.at[a, 10], tok_recv.at[a, 10], along_y(1 + 2 * a),
        ))
        wide[a, 1, a].wait_recv()
        ref = act_in.at[a, 1:4, lax.rem(x + 3 - 2 * a, 4), :, high]
        far[a, 1] = begin(remote(ref, ref, tok_send.at[a, 11], tok_recv.at[a, 11], along_x(1 + 2 * a)))

    def share_far(a):
        for axis in range(2):
            wide[a, axis, 1 - a].wait_recv()
            far[a, axis].wait_recv()
        share(a, 1)

    def multiply(q):
        for m in range(3):
            a = m // 2
            if m != 1 and q < 2:
                shares[a, q].wait_recv()
            ours, theirs = act_in[a, q].reshape(ROW, 512), act_px[a, q].reshape(ROW, 512)
            if q == 0:
                px_copies[m].wait_recv()
            if m == 2:
                part[q, m] = dot_nt(ours, w_d[0]) + dot_nt(theirs, px_d[...])
            else:
                part[q, m] = jnp.dot(ours, w_gu[0, m], preferred_element_type=F32) + jnp.dot(
                    theirs, px_gu[m], preferred_element_type=F32
                )

    def sum_copy(q, way, step):
        return remote(
            rs_send.at[q, way, step], rs_recv.at[q, way, step],
            rs_ssem.at[q, way, step], rs_rsem.at[q, way, step], ring(way),
        )

    def sum_ways(q, step):
        return (q % 2,) if step == 0 else (q % 2, 1 - q % 2)

    def reduce(q, step):
        for way in sum_ways(q, step):
            distance = 4 - step
            d = lax.rem(z + (distance if way == 0 else 8 - distance), 8)
            total = part[q, :, pl.ds(pl.multiple_of(d * SHARE, SHARE), SHARE)]
            if step > 0 and way in sum_ways(q, step - 1):
                sum_copy(q, way, step - 1).wait_recv()
                total += decode(rs_recv[q, way, step - 1])
            rs_send[q, way, step] = encode(total)
            sum_copy(q, way, step).start()

    def rows(q, d):
        return pl.ds(pl.multiple_of(q * ROW + d * SHARE, SHARE), SHARE)

    def activate(q):
        sums = part[q, :, pl.ds(pl.multiple_of(z * SHARE, SHARE), SHARE)]
        for way in sum_ways(q, 3):
            sum_copy(q, way, 3).wait_recv()
            sums += decode(rs_recv[q, way, 3])
        gate, up, grad_hidden = sums[0], sums[1], sums[2]
        sig = jax.nn.sigmoid(gate)
        silu_gate = gate * sig
        gathered[0, 0, rows(q, z)] = (silu_gate * up).astype(BF16)
        gathered[0, 1, rows(q, z)] = (grad_hidden * up * sig * (1.0 + gate * (1.0 - sig))).astype(BF16)
        gathered[0, 2, rows(q, z)] = (grad_hidden * silu_gate).astype(BF16)

    def spread_copy(q, way, step):
        ref = gathered.at[0, :, rows(q, lax.rem(z + (8 - step if way == 0 else step), 8))]
        return remote(ref, ref, ag_ssem.at[q, way, step], ag_rsem.at[q, way, step], ring(way))

    def spread_ways(q, step):
        return (q % 2,) if step == 3 else (q % 2, 1 - q % 2)

    def pair_copy(q, k):
        at = rows(q, lax.rem(z + (0, 7, 6, 5, 1, 2, 3, 4)[k], 8))
        return remote(
            gathered.at[0, :, at], gathered.at[1, :, at], pair_send.at[q, k], pair_recv.at[q, k], partner
        )

    def spread(q, step):
        if step == 0:
            activate(q)
        for way in (q % 2, 1 - q % 2):
            if 0 < step < 4 or (step == 4 and way == q % 2):
                spread_copy(q, way, step - 1).wait_recv()
            if step < 4 and way in spread_ways(q, step):
                spread_copy(q, way, step).start()
        if step == 0:
            pair_copy(q, 0).start()
        elif step < 4:
            pair_copy(q, step).start()
            pair_copy(q, 3 + step).start()
        else:
            pair_copy(q, 7).start()

    def gi_copy(q, d):
        return remote(
            gi_send.at[d, q], gi_recv.at[hid, lax.rem(d, 2)], gi_ssem.at[d, q],
            gi_rsem.at[hid, lax.rem(d, 2)], (mp, lax.rem(y + STEPS[q], 4) * 4 + d // 2),
        )

    def gi_each(q, d, act):
        if q == 0:
            pl.when(x != d // 2)(lambda: act(gi_copy(q, d)))
        else:
            act(gi_copy(q, d))

    def input_grad(distance):
        places = ((0, z),) if distance == 0 else ((7, lax.rem(z + 4, 8)),) if distance == 4 else (
            (distance, lax.rem(z + 8 - distance, 8)), (3 + distance, lax.rem(z + distance, 8))
        )
        for k, _ in places:
            for q in range(4):
                pair_copy(q, k).wait_recv()
        total = jnp.zeros((4 * SHARE * len(places), 512), F32)
        for half in range(2):
            for mat in range(2):
                left = jnp.concatenate([gathered[half, 1 + mat, rows(q, d)] for _, d in places for q in range(4)])
                total += dot_nt(left, w_gu[half, mat])
        for i, (_, d) in enumerate(places):
            for q in range(4):
                start = (4 * i + q) * SHARE
                gi_send[d, q] = encode(total[start : start + SHARE])
                gi_each(q, d, lambda copy: copy.start())

    def saliency_in(half, mat):
        tokens = act_in[0].reshape(512, 512)
        for cols in (slice(0, 512), slice(512, HALF)):
            grads = dot_tn(tokens, gathered[half, 1 + mat, :, cols])
            out_gu[half, mat, :, cols] = jnp.abs(w_gu[half, mat, :, cols].astype(F32) * grads).astype(BF16)

    def saliency_down(half):
        for cols in (slice(0, 512), slice(512, HALF)):
            grads = dot_tn(gathered[half, 0, :, cols], act_in[1].reshape(512, 512))
            out_d[half, cols, :] = jnp.abs(w_d[half, cols, :].astype(F32) * grads).astype(BF16)

    send_row(0)
    exchange(wd_ref.at[pl.ds(other_col, HALF), :], px_d)
    send_row(1)
    for copy in loads[2:]:
        copy.wait()
    load_half(1, other_col)
    events = [
        (4.0, 0, lambda: [copy.wait() for copy in loads[5:]]),
        (-0.05, 0, lambda: (send_column(0), send_column(1))),
        (0.9, 0, lambda: (pass_on(0), pass_on(1))),
        (1.9, 0, lambda: (share_far(0), share_far(1))),
    ]
    for q in range(4):
        events.append((START[q] - 0.1, q, lambda q=q: multiply(q)))
        for step in range(4):
            events.append((START[q] + step, q, lambda q=q, step=step: reduce(q, step)))
        for step in range(5):
            events.append((SPREAD[q] + step, q, lambda q=q, step=step: spread(q, step)))
    for distance, when in enumerate((1.05, 2.05, 3.05, 3.5, 4.5)):
        events.append((SPREAD[3] + when, 4, lambda distance=distance: input_grad(distance)))
    events.append((SPREAD[3] + 4.2, 4, lambda: (saliency_in(0, 0), saliency_in(0, 1))))
    for _, _, event in sorted(events, key=lambda e: e[:2]):
        event()
    saliency_down(0)
    for mat in range(2):
        saliency_in(1, mat)
    saliency_down(1)

    totals = [decode(gi_send[2 * x + i, 0]) for i in range(2)]
    for j in range(1, 16):
        slot = lax.rem(hid + j, 16)
        for i in range(2):
            remote(
                gi_send.at[0, 0], gi_recv.at[slot, i], gi_ssem.at[0, 0], gi_rsem.at[slot, i], in_plane(j)
            ).wait_recv()
            totals[i] += decode(gi_recv[slot, i])
    for i in range(2):
        gi_ref[SHARE * i : SHARE * i + SHARE] = totals[i].astype(BF16)

    for copy in copies:
        copy.wait_send()
    for q in range(4):
        for step in range(4):
            for way in sum_ways(q, step):
                sum_copy(q, way, step).wait_send()
            for way in spread_ways(q, step):
                spread_copy(q, way, step).wait_send()
        for k in range(8):
            pair_copy(q, k).wait_send()
        for d in range(8):
            gi_each(q, d, lambda copy: copy.wait_send())


def write_out(gi_in, gu_in, d_in, gi_ref, sg_ref, su_ref, sd_ref, sem):
    core = lax.rem(lax.axis_index("mp"), 2)
    copies = [pltpu.make_async_copy(gi_in, gi_ref, sem.at[6])]
    for half in range(2):
        at = pl.ds(pl.multiple_of((core + half * (1 - 2 * core)) * HALF, 128), HALF)
        for m, (src, dst) in enumerate((
            (gu_in.at[half, 0], sg_ref.at[:, at]),
            (gu_in.at[half, 1], su_ref.at[:, at]),
            (d_in.at[half], sd_ref.at[at, :]),
        )):
            copies.append(pltpu.make_async_copy(src, dst, sem.at[2 * m + half]))
    for copy in copies:
        copy.start()
    for copy in copies:
        copy.wait()


def local(tokens, grad_output, gate_weight, up_weight, down_weight):
    anywhere = pl.BlockSpec(memory_space=pl.ANY)
    dma = pltpu.SemaphoreType.DMA
    vmem = pl.BlockSpec(memory_space=pltpu.VMEM)
    results = pl.pallas_call(
        kernel,
        out_shape=(
            pltpu.VMEM((32, 512), BF16),
            pltpu.VMEM((2, 2, 512, HALF), BF16),
            pltpu.VMEM((2, HALF, 512), BF16),
        ),
        in_specs=[anywhere] * 5,
        out_specs=(vmem, vmem, vmem),
        scratch_shapes=[
            pltpu.VMEM((2, 4, 4, 32, 512), BF16),
            pltpu.VMEM((2, 4, 4, 32, 512), BF16),
            pltpu.VMEM((2, 2, 512, HALF), BF16),
            pltpu.VMEM((2, HALF, 512), BF16),
            pltpu.VMEM((2, 512, HALF), BF16),
            pltpu.VMEM((HALF, 512), BF16),
            pltpu.VMEM((4, 3, ROW, HALF), F32),
            pltpu.VMEM((4, 2, 4, 3, SHARE, HALF), BF16),
            pltpu.VMEM((4, 2, 4, 3, SHARE, HALF), BF16),
            pltpu.VMEM((2, 3, 512, HALF), BF16),
            pltpu.VMEM((8, 4, SHARE, 512), BF16),
            pltpu.VMEM((16, 2, SHARE, 512), BF16),
            dma((8,)),
            dma((3,)),
            dma((3,)),
            dma((2, 12)),
            dma((2, 12)),
            dma((2, 2)),
            dma((2, 2)),
            dma((4, 2, 4)),
            dma((4, 2, 4)),
            dma((4, 2, 4)),
            dma((4, 2, 4)),
            dma((4, 8)),
            dma((4, 8)),
            dma((8, 4)),
            dma((16, 2)),
        ],
        compiler_params=pltpu.CompilerParams(
            collective_id=0, has_side_effects=True, vmem_limit_bytes=55 * 2**20
        ),
        cost_estimate=pl.CostEstimate(flops=7_516_192_768, bytes_accessed=11_010_048, transcendentals=2_000_000),
    )(tokens, grad_output, gate_weight, up_weight, down_weight)
    return pl.pallas_call(
        write_out,
        out_shape=(
            jax.ShapeDtypeStruct((32, 512), BF16),
            jax.ShapeDtypeStruct((512, 1792), BF16),
            jax.ShapeDtypeStruct((512, 1792), BF16),
            jax.ShapeDtypeStruct((1792, 512), BF16),
        ),
        in_specs=[anywhere] * 3,
        out_specs=(anywhere,) * 4,
        scratch_shapes=[dma((7,))],
        compiler_params=pltpu.CompilerParams(vmem_limit_bytes=2**20),
    )(*results)


def solution(mesh):
    return jax.shard_map(
        local,
        mesh=mesh,
        in_specs=(
            P("hidden", "mp"),
            P("hidden", "mp"),
            P("mp", "hidden"),
            P("mp", "hidden"),
            P("hidden", "mp"),
        ),
        out_specs=(P("hidden", "mp"), P("mp", "hidden"), P("mp", "hidden"), P("hidden", "mp")),
        check_vma=False,
    )
```
